32 devices in a mesh: frame: 16 (over z, x, core), patch: 2 (over y).
Axes of the slice: x: 2, y: 2, z: 4, core: 2. Of those that a mesh axis runs over, the one named last changes fastest.
Arguments:
- clip: bfloat16 [4, 16, 256, 1280], P(None, 'frame', 'patch'), may hold values from -54 to 54
- norm_time: float32 [1280], replicated, may hold values from 0.1 to 1.9
- w_time_qkv: bfloat16 [1280, 1920], replicated, may hold values from -0.15625 to 0.15625
- q_gain_time: float32 [640], replicated, may hold values from 1 to 2
- k_gain_time: float32 [640], replicated, may hold values from 1 to 2
- w_time_out: bfloat16 [640, 1280], replicated, may hold values from -0.25 to 0.25
- norm_space: float32 [1280], replicated, may hold values from 0.1 to 1.9
- w_space_qkv: bfloat16 [1280, 1920], replicated, may hold values from -0.15625 to 0.15625
- q_gain_space: float32 [640], replicated, may hold values from 1 to 2
- k_gain_space: float32 [640], replicated, may hold values from 1 to 2
Outputs:
- spatial_out: bfloat16 [4, 16, 256, 640], P(None, 'frame', 'patch')
The draws below stay inside these ranges and needn't reach their ends.
All inputs are finite; a program needn't handle non-finite values.
Results may differ from the reference program's by a relative error of at most 0.025.
Values may be sent and summed in bfloat16 or wider, within the bound.
No kernel may reach another device: no remote copies, remote signals or barrier semaphores. Data moves between devices by JAX's collectives and lax.ppermute only.
A program may use at most 128 MiB of HBM per device.

```python
import math
import jax
import jax.numpy as jnp
from jax import lax

D = 1280
HEADS = 8
HDIM = 80
CLIPS = 4
FRAMES = 16
PATCHES = 256


def draw_clip(key, part):
    key = jax.random.fold_in(key, 7)
    key_base = jax.random.fold_in(key, 1)
    key_rows = jax.random.fold_in(key, 2)
    key_cols = jax.random.fold_in(key, 3)
    full_shape = (CLIPS, FRAMES, PATCHES, D)
    low = math.log(0.3)
    high = math.log(3.0)
    row_scale = jnp.exp(jax.random.uniform(key_rows, (CLIPS, FRAMES, PATCHES, 1), jnp.float32, low, high))
    col_scale = jnp.exp(jax.random.uniform(key_cols, (D,), jnp.float32, low, high))
    base = jnp.clip(jax.random.normal(key_base, full_shape, jnp.float32), -6.0, 6.0)
    return (base * row_scale * col_scale).astype(jnp.bfloat16)


def noise(rng, shape, width, reach, kind=jnp.bfloat16):
    array = jax.random.normal(rng, shape, jnp.float32) * width
    return jnp.minimum(jnp.maximum(array, -reach), reach).astype(kind)


def setup_inputs(seed: int = 0) -> dict:
    seeds = jax.random.split(jax.random.key(seed), 11)
    clip = draw_clip(jax.random.fold_in(seeds[10], 71), 0)
    norm_time = jnp.clip(1.0 + 0.18 * jax.random.normal(seeds[1], (D,), jnp.float32), 0.1, 1.9)
    w_time_qkv = noise(seeds[2], (D, 3 * HEADS * HDIM), D ** -0.5, 0.15625)
    q_gain_time = jnp.clip(jax.random.uniform(seeds[3], (HEADS * HDIM,), jnp.float32, 1.0, 2.0), 1.0, 2.0)
    k_gain_time = jnp.clip(jax.random.uniform(seeds[4], (HEADS * HDIM,), jnp.float32, 1.0, 2.0), 1.0, 2.0)
    w_time_out = noise(seeds[5], (HEADS * HDIM, D), (HEADS * HDIM) ** -0.5, 0.25)
    norm_space = jnp.clip(1.0 + 0.18 * jax.random.normal(seeds[6], (D,), jnp.float32), 0.1, 1.9)
    w_space_qkv = noise(seeds[7], (D, 3 * HEADS * HDIM), D ** -0.5, 0.15625)
    q_gain_space = jnp.clip(jax.random.uniform(seeds[8], (HEADS * HDIM,), jnp.float32, 1.0, 2.0), 1.0, 2.0)
    k_gain_space = jnp.clip(jax.random.uniform(seeds[9], (HEADS * HDIM,), jnp.float32, 1.0, 2.0), 1.0, 2.0)
    return dict(clip=clip, norm_time=norm_time, w_time_qkv=w_time_qkv, q_gain_time=q_gain_time, k_gain_time=k_gain_time, w_time_out=w_time_out, norm_space=norm_space, w_space_qkv=w_space_qkv, q_gain_space=q_gain_space, k_gain_space=k_gain_space)


epsilon = 1e-06

def layer_norm(token_rows, norm_gain):
    values = token_rows.astype(jnp.float32)
    average = lax.optimization_barrier(jnp.mean(values, axis=-1, keepdims=True))
    centred = values - average
    variance = lax.optimization_barrier(jnp.mean(centred * centred, axis=-1, keepdims=True))
    return (centred * lax.rsqrt(variance + epsilon) * norm_gain).astype(jnp.bfloat16)

def head_norm(projected, head_gain, head_size):
    leading = projected.shape[:-1]
    split_heads = projected.reshape(leading + (projected.shape[-1] // head_size, head_size))
    squares = lax.optimization_barrier(jnp.mean(split_heads * split_heads, axis=-1, keepdims=True))
    scaled = split_heads * lax.rsqrt(squares + epsilon)
    return (scaled.reshape(projected.shape) * head_gain).astype(jnp.bfloat16)

def project_heads(normed, weight, query_gain, key_gain, head_size):
    inner_width = weight.shape[1] // 3
    product = jnp.dot(normed, weight, preferred_element_type=jnp.float32)
    query = head_norm(product[:, :inner_width], query_gain, head_size)
    keys = head_norm(product[:, inner_width:2 * inner_width], key_gain, head_size)
    values = product[:, 2 * inner_width:].astype(jnp.bfloat16)
    return (query, keys, values)

def time_attention(query, keys, values):
    clip_count, frame_count, patch_count, inner_width = query.shape
    split = (clip_count, frame_count, patch_count, inner_width // HDIM, HDIM)
    query_heads = query.reshape(split).astype(jnp.float32)
    key_heads = keys.reshape(split).astype(jnp.float32)
    value_heads = values.reshape(split).astype(jnp.float32)
    scores = jnp.einsum('cfphd,cgphd->cphfg', query_heads, key_heads) * HDIM ** (-0.5)
    exponent = jnp.exp(scores)
    totals = lax.optimization_barrier(jnp.sum(exponent, axis=-1))
    rounded = lax.optimization_barrier(exponent.astype(jnp.bfloat16))
    summed = jnp.einsum('cphfg,cgphd->cfphd', rounded.astype(jnp.float32), value_heads)
    result = summed / jnp.transpose(totals, (0, 3, 1, 2))[..., None]
    return result.reshape(query.shape).astype(jnp.bfloat16)

def space_frame(inputs):
    query, keys, values = inputs
    patch_count, inner_width = query.shape
    split = (patch_count, inner_width // HDIM, HDIM)
    query_heads = query.reshape(split).astype(jnp.float32)
    key_heads = keys.reshape(split).astype(jnp.float32)
    value_heads = values.reshape(split).astype(jnp.float32)
    scores = jnp.einsum('qhd,khd->hqk', query_heads, key_heads) * HDIM ** (-0.5)
    exponent = jnp.exp(scores)
    totals = lax.optimization_barrier(jnp.sum(exponent, axis=-1))
    rounded = lax.optimization_barrier(exponent.astype(jnp.bfloat16))
    summed = jnp.einsum('hqk,khd->qhd', rounded.astype(jnp.float32), value_heads)
    result = summed / jnp.transpose(totals, (1, 0))[..., None]
    return result.reshape(query.shape).astype(jnp.bfloat16)

def reference(clip, norm_time, w_time_qkv, q_gain_time, k_gain_time, w_time_out, norm_space, w_space_qkv, q_gain_space, k_gain_space):
    inner_width = w_time_out.shape[0]
    token_rows = clip.reshape(-1, D)
    normed = layer_norm(token_rows, norm_time)
    query, keys, values = project_heads(normed, w_time_qkv, q_gain_time, k_gain_time, HDIM)
    attn_shape = (CLIPS, FRAMES, PATCHES, inner_width)
    attended = time_attention(query.reshape(attn_shape), keys.reshape(attn_shape), values.reshape(attn_shape))
    delta = jnp.dot(attended.reshape(-1, inner_width), w_time_out, preferred_element_type=jnp.float32)
    mixed = (token_rows.astype(jnp.float32) + delta).astype(jnp.bfloat16)
    space_normed = layer_norm(mixed, norm_space)
    space_query, space_keys, space_values = project_heads(space_normed, w_space_qkv, q_gain_space, k_gain_space, HDIM)
    frame_shape = (CLIPS * FRAMES, PATCHES, inner_width)
    spatial = lax.map(space_frame, (space_query.reshape(frame_shape), space_keys.reshape(frame_shape), space_values.reshape(frame_shape)))
    return spatial.reshape(attn_shape)
```

```python
import functools

import jax
import jax.numpy as jnp
from jax import lax
from jax.experimental import pallas as pl
from jax.experimental.pallas import tpu as pltpu
from jax.sharding import PartitionSpec as P

HDIM = 80
LANES = 128
EPS = 1e-06
CELLS = 16
MIB = 1024 * 1024

VMEM = pl.BlockSpec(memory_space=pltpu.VMEM)
ANY = pl.BlockSpec(memory_space=pl.ANY)


def layer_norm(values, norm_gain):
    average = jnp.mean(values, axis=-1, keepdims=True)
    centred = values - average
    variance = jnp.mean(centred * centred, axis=-1, keepdims=True)
    return (centred * lax.rsqrt(variance + EPS) * norm_gain).astype(jnp.bfloat16)


def head_norm(part, gain, ones):
    sums = jnp.dot((part * part).astype(jnp.bfloat16), ones, preferred_element_type=jnp.float32)
    return (part * lax.rsqrt(sums * (1.0 / HDIM) + EPS) * gain).astype(jnp.bfloat16)


def lanes_of(head, tile, rows):
    lane = lax.broadcasted_iota(jnp.int32, (rows, LANES), 1) + tile * LANES
    return (lane >= head * HDIM) & (lane < (head + 1) * HDIM)


def attend(query, load_keys, load_values, inner, keep):
    rows = query.shape[0]
    tiles = [None] * (inner // LANES)
    for head in range(inner // HDIM):
        first, last = head * HDIM // LANES, ((head + 1) * HDIM - 1) // LANES
        lo, hi = first * LANES, (last + 1) * LANES
        masks = [lanes_of(head, tile, rows) for tile in range(first, last + 1)]
        own = jnp.concatenate(
            [
                jnp.where(mask, query[:, t * LANES : (t + 1) * LANES], jnp.zeros((), query.dtype))
                for mask, t in zip(masks, range(first, last + 1))
            ],
            axis=1,
        )
        scores = lax.dot_general(
            own, load_keys(lo, hi), (((1,), (1,)), ((), ())), preferred_element_type=jnp.float32
        )
        exponent = jnp.exp(scores * HDIM ** (-0.5))
        if keep is not None:
            exponent = jnp.where(keep, exponent, 0.0)
        total = jnp.sum(exponent, axis=-1, keepdims=True)
        summed = jnp.dot(
            exponent.astype(jnp.bfloat16), load_values(lo, hi), preferred_element_type=jnp.float32
        )
        result = summed * (1.0 / total)
        for i, t in enumerate(range(first, last + 1)):
            piece = result[:, i * LANES : (i + 1) * LANES]
            tiles[t] = piece if tiles[t] is None else jnp.where(masks[i], piece, tiles[t])
    return jnp.concatenate(tiles, axis=1)


def partner_rows(k, cells):
    chip = lax.axis_index("frame") // 2
    return pl.ds(pl.multiple_of((chip ^ k) * cells, cells), cells)


def pack_kernel(cells, x_ref, *out_refs):
    for k, out_ref in enumerate(out_refs):
        out_ref[...] = x_ref[partner_rows(k, cells), :]


def time_kernel(count, *refs):
    pieces, weights, (q_ref, kv_ref) = refs[:count], refs[count : count + 5], refs[-2:]
    norm_ref, w_ref, qg_ref, kg_ref, ones_ref = weights
    inner = w_ref.shape[1] // 3
    normed = jnp.concatenate(
        [layer_norm(ref[...].astype(jnp.float32), norm_ref[...]) for ref in pieces], axis=0
    )
    product = jnp.dot(normed, w_ref[...], preferred_element_type=jnp.float32)
    query = head_norm(product[:, :inner], qg_ref[...], ones_ref[...])
    keys = head_norm(product[:, inner : 2 * inner], kg_ref[...], ones_ref[...])
    shape = q_ref.shape
    q_ref[...] = query.reshape(shape)
    kv_ref[0] = keys.reshape(shape)
    kv_ref[1] = product[:, 2 * inner :].astype(jnp.bfloat16).reshape(shape)


def time_attention_kernel(parts, *refs):
    queries, held, outs = refs[:parts], refs[parts : 3 * parts], refs[3 * parts + 1 :]
    cells = queries[0].shape[1]
    inner = queries[0].shape[2]
    rows = len(outs) * CELLS
    row = lax.broadcasted_iota(jnp.int32, (rows, 2 * rows), 0)
    col = lax.broadcasted_iota(jnp.int32, (rows, 2 * rows), 1)
    keep = lax.rem(row, CELLS) == lax.rem(col, CELLS)
    for b in range(cells // CELLS):
        at = slice(b * CELLS, (b + 1) * CELLS)
        query = jnp.concatenate([ref[:, at, :] for ref in queries], axis=0)

        def load(which):
            def columns(lo, hi):
                blocks = [ref[which, :, at, lo:hi] for ref in held]
                return jnp.concatenate(blocks, axis=0).reshape(2 * rows, hi - lo)

            return columns

        result = attend(query.reshape(rows, inner), load(0), load(1), inner, keep)
        result = result.astype(jnp.bfloat16).reshape(len(outs), CELLS, inner)
        for i, out in enumerate(outs):
            out[at, :] = result[i]


def gather_kernel(count, *refs):
    pieces, out_ref = refs[:count], refs[-1]
    cells = pieces[0].shape[0]
    chip = lax.axis_index("frame") // 2
    for j, ref in enumerate(pieces):
        at = lax.rem(chip, count) ^ j
        out_ref[pl.ds(pl.multiple_of(at * cells, cells), cells), :] = ref[...]


def clip_of(group, count):
    return (lax.axis_index("frame") // 2 // count) ^ group


def space_rows(blocks, clips, where, with_query, weights):
    wo_ref, norm_ref, w_ref, qg_ref, kg_ref, ones_ref = weights
    patches, inner = blocks[0].shape
    at = pl.ds(pl.multiple_of(where * patches, patches), patches)
    normed = []
    for block, clip_ref in zip(blocks, clips):
        delta = jnp.dot(block[...], wo_ref[...], preferred_element_type=jnp.float32)
        own = clip_ref[at, :].astype(jnp.float32)
        mixed = (own + delta).astype(jnp.bfloat16).astype(jnp.float32)
        normed.append(layer_norm(mixed, norm_ref[...]))
    query = None
    if with_query:
        product = jnp.dot(normed[0], w_ref[:, :inner], preferred_element_type=jnp.float32)
        query = head_norm(product, qg_ref[...], ones_ref[...])
    normed = jnp.concatenate(normed, axis=0)
    product = jnp.dot(normed, w_ref[:, inner:], preferred_element_type=jnp.float32)
    keys = head_norm(product[:, :inner], kg_ref[...], ones_ref[...])
    return query, keys, product[:, inner:].astype(jnp.bfloat16)


def space_clip_kernel(group, count, sides, *refs):
    blocks, clips, refs = refs[:sides], refs[sides : 2 * sides], refs[2 * sides :]
    weights, out_ref = refs[:6], refs[6]
    query, keys, values = space_rows(blocks, clips, clip_of(group, count), True, weights)
    inner = out_ref.shape[1]
    result = attend(
        query, lambda lo, hi: keys[:, lo:hi], lambda lo, hi: values[:, lo:hi], inner, None
    )
    out_ref[...] = result.astype(jnp.bfloat16)


def space_own_kernel(group, count, block_ref, clip_ref, *refs):
    weights, (q_ref, k_ref, v_ref) = refs[:6], refs[6:]
    q_ref[...], k_ref[...], v_ref[...] = space_rows(
        [block_ref], [clip_ref], clip_of(group, count), True, weights
    )


def space_last_kernel(group, count, others, *refs):
    blocks, clips, refs = refs[:others], refs[others : 2 * others], refs[2 * others :]
    weights, own, done, out_ref = refs[:6], refs[6:9], refs[9:-1], refs[-1]
    inner = out_ref.shape[2]
    for g, ref in enumerate(done):
        out_ref[clip_of(g, count)] = ref[...]
    where = clip_of(group, count)
    _, keys, values = space_rows(blocks, clips, where, False, weights)
    q_ref, k_ref, v_ref = own
    result = attend(
        q_ref[...],
        lambda lo, hi: jnp.concatenate([k_ref[:, lo:hi], keys[:, lo:hi]], axis=0),
        lambda lo, hi: jnp.concatenate([v_ref[:, lo:hi], values[:, lo:hi]], axis=0),
        inner,
        None,
    )
    out_ref[where] = result.astype(jnp.bfloat16)


def from_sides(array, size):
    return [
        lax.ppermute(array, "patch", [(i, (i - hop) % size) for i in range(size)])
        for hop in range(1, size)
    ]


def call(kernel, name, outs, operands, any_last=0, scratch=(), mebibytes=20, flops=0):
    bf16 = jnp.bfloat16
    shapes = [jax.ShapeDtypeStruct(shape, bf16) for shape in outs]
    results = pl.pallas_call(
        kernel,
        out_shape=shapes,
        in_specs=[VMEM] * (len(operands) - any_last) + [ANY] * any_last,
        out_specs=[VMEM] * len(outs),
        scratch_shapes=[pltpu.VMEM(shape, bf16) for shape in scratch],
        compiler_params=pltpu.CompilerParams(vmem_limit_bytes=mebibytes * MIB),
        cost_estimate=pl.CostEstimate(flops=flops, bytes_accessed=MIB, transcendentals=0),
        name=name,
    )(*operands)
    return list(results)


def body(
    sizes,
    clip,
    norm_time,
    w_time_qkv,
    q_gain_time,
    k_gain_time,
    w_time_out,
    norm_space,
    w_space_qkv,
    q_gain_space,
    k_gain_space,
):
    frames, sides = sizes
    clips, _, patches, features = clip.shape
    inner = w_time_out.shape[0]
    tokens = clips * patches
    chips = frames // 2
    cells = tokens // chips
    half = chips // 2
    count = chips // clips
    bf16 = jnp.bfloat16
    head = jnp.arange(inner) // HDIM
    ones = (head[:, None] == head[None, :]).astype(bf16)
    near, far = list(range(half)), list(range(half, chips))
    project = 2 * (tokens // 2) * features * 3 * inner * 2

    def exchange(pieces):
        moved = {0: pieces[0]}
        for k in range(1, chips):
            moved[k] = lax.ppermute(pieces[k], "frame", [(i, i ^ (2 * k)) for i in range(frames)])
        return moved

    def other_core(array):
        return lax.ppermute(array, "frame", [(i, i ^ 1) for i in range(frames)])

    rows = clip.reshape(tokens, features)
    clip_sides = [rows] + from_sides(rows, sides)
    pieces = call(
        functools.partial(pack_kernel, cells), "pack", [(cells, features)] * chips, [rows]
    )
    moved = exchange(pieces)

    time_weights = [
        norm_time.reshape(1, -1),
        w_time_qkv,
        q_gain_time.reshape(1, -1),
        k_gain_time.reshape(1, -1),
        ones,
    ]
    queries, held = [], []
    for members, name in ((near, "time_near"), (far, "time_far")):
        query, key_value = call(
            functools.partial(time_kernel, len(members)),
            name,
            [(len(members), cells, inner), (2, len(members), cells, inner)],
            [moved[k] for k in members] + time_weights + queries,
            any_last=len(queries),
            flops=project,
        )
        queries.append(query)
        held += [key_value, other_core(key_value)]
    attended = call(
        functools.partial(time_attention_kernel, 2),
        "time_attention",
        [(cells, inner)] * chips,
        queries + held + [clip_sides[-1]],
        any_last=1,
        flops=project,
    )

    back = exchange(attended)
    space_weights = [
        w_time_out,
        norm_space.reshape(1, -1),
        w_space_qkv,
        q_gain_space.reshape(1, -1),
        k_gain_space.reshape(1, -1),
        ones,
    ]
    room = 24 + 8 * (sides - 2)
    block_shape = (patches, inner)
    done = []
    for g in range(clips):
        pieces = [back[g * count + j] for j in range(count)]
        before = done[g - 2 : g - 1] if g >= 2 else []
        (block,) = call(
            functools.partial(gather_kernel, count),
            "gather",
            [block_shape],
            pieces + before,
            any_last=len(before),
        )
        others = from_sides(block, sides)
        if g < clips - 1:
            done += call(
                functools.partial(space_clip_kernel, g, count, sides),
                "space_clip",
                [block_shape],
                [block] + others + clip_sides + space_weights,
                mebibytes=room,
                flops=project,
            )
    own = call(
        functools.partial(space_own_kernel, clips - 1, count),
        "space_own",
        [block_shape] * 3,
        [block, rows] + space_weights,
        mebibytes=room,
        flops=project // 2,
    )
    (spatial,) = call(
        functools.partial(space_last_kernel, clips - 1, count, sides - 1),
        "space_last",
        [(clips, patches, inner)],
        others + clip_sides[1:] + space_weights + own + done,
        mebibytes=room,
        flops=project // 2,
    )
    return spatial.reshape(clips, 1, patches, inner)


def solution(mesh):
    sizes = (mesh.shape["frame"], mesh.shape["patch"])
    in_specs = (P(None, "frame", "patch", None),) + (P(),) * 9
    out_specs = P(None, "frame", "patch", None)
    return jax.shard_map(
        functools.partial(body, sizes),
        mesh=mesh,
        in_specs=in_specs,
        out_specs=out_specs,
        check_vma=False,
    )
```

```python
import functools

import jax
import jax.numpy as jnp
from jax import lax
from jax.experimental import pallas as pl
from jax.experimental.pallas import tpu as pltpu
from jax.sharding import PartitionSpec as P

HDIM = 80
LANES = 128
EPS = 1e-06
CELLS = 16
MIB = 1024 * 1024

VMEM = pl.BlockSpec(memory_space=pltpu.VMEM)
ANY = pl.BlockSpec(memory_space=pl.ANY)


def layer_norm(values, norm_gain):
    average = jnp.mean(values, axis=-1, keepdims=True)
    centred = values - average
    variance = jnp.mean(centred * centred, axis=-1, keepdims=True)
    return (centred * lax.rsqrt(variance + EPS) * norm_gain).astype(jnp.bfloat16)


def head_norm(part, gain, ones):
    sums = jnp.dot((part * part).astype(jnp.bfloat16), ones, preferred_element_type=jnp.float32)
    return (part * lax.rsqrt(sums * (1.0 / HDIM) + EPS) * gain).astype(jnp.bfloat16)


def lanes_of(head, tile, rows):
    lane = lax.broadcasted_iota(jnp.int32, (rows, LANES), 1) + tile * LANES
    return (lane >= head * HDIM) & (lane < (head + 1) * HDIM)


def attend(query, load_keys, load_values, inner, keep):
    rows = query.shape[0]
    spans, masks, scores, exponents, totals = [], [], [], [], []
    for head in range(inner // HDIM):
        first, last = head * HDIM // LANES, ((head + 1) * HDIM - 1) // LANES
        spans.append((first, last + 1))
        masks.append([lanes_of(head, tile, rows) for tile in range(first, last + 1)])
        own = [
            jnp.where(mask, query[:, t * LANES : (t + 1) * LANES], jnp.zeros((), query.dtype))
            for mask, t in zip(masks[-1], range(first, last + 1))
        ]
        keys = load_keys(first * LANES, (last + 1) * LANES)
        scores.append(
            lax.dot_general(
                jnp.concatenate(own, axis=1),
                keys,
                (((1,), (1,)), ((), ())),
                preferred_element_type=jnp.float32,
            )
        )
    for score in scores:
        exponent = jnp.exp(score * HDIM ** (-0.5))
        if keep is not None:
            exponent = jnp.where(keep, exponent, 0.0)
        totals.append(jnp.sum(exponent, axis=-1, keepdims=True))
        exponents.append(exponent.astype(jnp.bfloat16))
    tiles = [None] * (inner // LANES)
    for (first, end), mask, exponent, total in zip(spans, masks, exponents, totals):
        values = load_values(first * LANES, end * LANES)
        summed = jnp.dot(exponent, values, preferred_element_type=jnp.float32)
        result = summed * (1.0 / total)
        for i, t in enumerate(range(first, end)):
            piece = result[:, i * LANES : (i + 1) * LANES]
            tiles[t] = piece if tiles[t] is None else jnp.where(mask[i], piece, tiles[t])
    return jnp.concatenate(tiles, axis=1)


def partner_rows(k, cells):
    chip = lax.axis_index("frame") // 2
    return pl.ds(pl.multiple_of((chip ^ k) * cells, cells), cells)


def pack_kernel(cells, x_ref, *out_refs):
    for k, out_ref in enumerate(out_refs):
        out_ref[...] = x_ref[partner_rows(k, cells), :]


def time_kernel(count, *refs):
    pieces, weights, (q_ref, kv_ref) = refs[:count], refs[count : count + 5], refs[-2:]
    norm_ref, w_ref, qg_ref, kg_ref, ones_ref = weights
    inner = w_ref.shape[1] // 3
    normed = jnp.concatenate(
        [layer_norm(ref[...].astype(jnp.float32), norm_ref[...]) for ref in pieces], axis=0
    )
    product = jnp.dot(normed, w_ref[...], preferred_element_type=jnp.float32)
    query = head_norm(product[:, :inner], qg_ref[...], ones_ref[...])
    keys = head_norm(product[:, inner : 2 * inner], kg_ref[...], ones_ref[...])
    shape = q_ref.shape
    q_ref[...] = query.reshape(shape)
    kv_ref[0] = keys.reshape(shape)
    kv_ref[1] = product[:, 2 * inner :].astype(jnp.bfloat16).reshape(shape)


def time_attention_kernel(parts, *refs):
    queries, held, outs = refs[:2], refs[2:6], refs[7:]
    count, cells, inner = outs[0].shape
    rows = count * len(outs) * CELLS
    row = lax.broadcasted_iota(jnp.int32, (rows, 2 * rows), 0)
    col = lax.broadcasted_iota(jnp.int32, (rows, 2 * rows), 1)
    keep = lax.rem(row, CELLS) == lax.rem(col, CELLS)
    for b in range(cells // CELLS):
        at = slice(b * CELLS, (b + 1) * CELLS)
        query = jnp.concatenate([ref[:, at, :] for ref in queries], axis=0).reshape(rows, inner)

        def load(which):
            def columns(lo, hi):
                blocks = [ref[which, :, at, lo:hi] for ref in held]
                return jnp.concatenate(blocks, axis=0).reshape(2 * rows, hi - lo)

            return columns

        result = attend(query, load(0), load(1), inner, keep).astype(jnp.bfloat16)
        for i, k in enumerate(parts[0] + parts[1]):
            outs[k // count][k % count, at, :] = result[i * CELLS : (i + 1) * CELLS]


def gather_kernel(count, *refs):
    pieces, out_ref = refs[:count], refs[-1]
    cells = pieces[0].shape[0]
    chip = lax.axis_index("frame") // 2
    for j, ref in enumerate(pieces):
        at = lax.rem(chip, count) ^ j
        out_ref[pl.ds(pl.multiple_of(at * cells, cells), cells), :] = ref[...]


def relay_kernel(which, landed_ref, *refs):
    refs[-1][...] = landed_ref[which]


def clip_of(group, count):
    return (lax.axis_index("frame") // 2 // count) ^ group


def space_rows(blocks, clips, where, with_query, weights):
    wo_ref, norm_ref, w_ref, qg_ref, kg_ref, ones_ref = weights
    patches, inner = blocks[0].shape
    at = pl.ds(pl.multiple_of(where * patches, patches), patches)
    normed = []
    for block, clip_ref in zip(blocks, clips):
        delta = jnp.dot(block[...], wo_ref[...], preferred_element_type=jnp.float32)
        own = clip_ref[at, :].astype(jnp.float32)
        mixed = (own + delta).astype(jnp.bfloat16).astype(jnp.float32)
        normed.append(layer_norm(mixed, norm_ref[...]))
    query = None
    if with_query:
        product = jnp.dot(normed[0], w_ref[:, :inner], preferred_element_type=jnp.float32)
        query = head_norm(product, qg_ref[...], ones_ref[...])
    normed = jnp.concatenate(normed, axis=0)
    product = jnp.dot(normed, w_ref[:, inner:], preferred_element_type=jnp.float32)
    keys = head_norm(product[:, :inner], kg_ref[...], ones_ref[...])
    return query, keys, product[:, inner:].astype(jnp.bfloat16)


def space_clip_kernel(group, count, sides, *refs):
    blocks, clips, refs = refs[:sides], refs[sides : 2 * sides], refs[2 * sides :]
    weights, out_ref = refs[:6], refs[-1]
    query, keys, values = space_rows(blocks, clips, clip_of(group, count), True, weights)
    inner = out_ref.shape[1]
    result = attend(
        query, lambda lo, hi: keys[:, lo:hi], lambda lo, hi: values[:, lo:hi], inner, None
    )
    out_ref[...] = result.astype(jnp.bfloat16)


def space_own_kernel(group, count, block_ref, clip_ref, *refs):
    weights, (q_ref, k_ref, v_ref) = refs[:6], refs[6:]
    q_ref[...], k_ref[...], v_ref[...] = space_rows(
        [block_ref], [clip_ref], clip_of(group, count), True, weights
    )


def space_last_kernel(order, count, others, *refs):
    blocks, clips, refs = refs[:others], refs[others : 2 * others], refs[2 * others :]
    weights, own, done, out_ref = refs[:6], refs[6:9], refs[9:-1], refs[-1]
    inner = out_ref.shape[2]
    for g, ref in zip(order, done):
        out_ref[clip_of(g, count)] = ref[...]
    where = clip_of(order[-1], count)
    _, keys, values = space_rows(blocks, clips, where, False, weights)
    q_ref, k_ref, v_ref = own
    result = attend(
        q_ref[...],
        lambda lo, hi: jnp.concatenate([k_ref[:, lo:hi], keys[:, lo:hi]], axis=0),
        lambda lo, hi: jnp.concatenate([v_ref[:, lo:hi], values[:, lo:hi]], axis=0),
        inner,
        None,
    )
    out_ref[where] = result.astype(jnp.bfloat16)


def from_sides(array, size):
    return [
        lax.ppermute(array, "patch", [(i, (i - hop) % size) for i in range(size)])
        for hop in range(1, size)
    ]


def call(kernel, name, outs, operands, any_last=0, scratch=(), mebibytes=20, flops=0):
    bf16 = jnp.bfloat16
    shapes = [jax.ShapeDtypeStruct(shape, bf16) for shape in outs]
    results = pl.pallas_call(
        kernel,
        out_shape=shapes,
        in_specs=[VMEM] * (len(operands) - any_last) + [ANY] * any_last,
        out_specs=[VMEM] * len(outs),
        scratch_shapes=[pltpu.VMEM(shape, bf16) for shape in scratch],
        compiler_params=pltpu.CompilerParams(vmem_limit_bytes=mebibytes * MIB),
        cost_estimate=pl.CostEstimate(flops=flops, bytes_accessed=MIB, transcendentals=0),
        name=name,
    )(*operands)
    return list(results)


def body(
    sizes,
    clip,
    norm_time,
    w_time_qkv,
    q_gain_time,
    k_gain_time,
    w_time_out,
    norm_space,
    w_space_qkv,
    q_gain_space,
    k_gain_space,
):
    frames, sides = sizes
    clips, _, patches, features = clip.shape
    inner = w_time_out.shape[0]
    tokens = clips * patches
    chips = frames // 2
    cells = tokens // chips
    half = chips // 2
    count = chips // clips
    bf16 = jnp.bfloat16
    head = jnp.arange(inner) // HDIM
    ones = (head[:, None] == head[None, :]).astype(bf16)
    quarter = max(1, half // 2)
    parts = [
        list(range(half, half + quarter)) + list(range(quarter)),
        list(range(half + quarter, chips)) + list(range(quarter, half)),
    ]
    order = list(range(clips))
    project = 2 * (tokens // 2) * features * 3 * inner * 2

    def exchange(pieces):
        moved = {0: pieces[0]}
        for k in parts[0] + parts[1]:
            if k:
                pairs = [(i, i ^ (2 * k)) for i in range(frames)]
                moved[k] = lax.ppermute(pieces[k], "frame", pairs)
        return moved

    def other_core(array):
        return lax.ppermute(array, "frame", [(i, i ^ 1) for i in range(frames)])

    rows = clip.reshape(tokens, features)
    clip_sides = [rows] + from_sides(rows, sides)
    pieces = call(
        functools.partial(pack_kernel, cells), "pack", [(cells, features)] * chips, [rows]
    )
    moved = exchange(pieces)

    time_weights = [
        norm_time.reshape(1, -1),
        w_time_qkv,
        q_gain_time.reshape(1, -1),
        k_gain_time.reshape(1, -1),
        ones,
    ]
    queries, held = [], []
    for members, name in zip(parts, ("time_first", "time_second")):
        query, key_value = call(
            functools.partial(time_kernel, len(members)),
            name,
            [(len(members), cells, inner), (2, len(members), cells, inner)],
            [moved[k] for k in members] + time_weights + queries,
            any_last=len(queries),
            flops=project,
        )
        queries.append(query)
        held += [key_value, other_core(key_value)]
    attended = call(
        functools.partial(time_attention_kernel, parts),
        "time_attention",
        [(count, cells, inner)] * clips,
        queries + held + [clip_sides[-1]],
        any_last=1,
        flops=project,
    )

    def step_to(array, k):
        return lax.ppermute(array, "frame", [(i, i ^ (2 * k)) for i in range(frames)])

    landed = {g: step_to(attended[g], g * count) if g else attended[0] for g in order}
    space_weights = [
        w_time_out,
        norm_space.reshape(1, -1),
        w_space_qkv,
        q_gain_space.reshape(1, -1),
        k_gain_space.reshape(1, -1),
        ones,
    ]
    room = 24 + 8 * (sides - 2)
    block_shape = (patches, inner)
    done = []
    for step, g in enumerate(order):
        pieces = [landed[g][0]]
        before = done[1:2] if step >= 2 else []
        for j in range(1, count):
            relayed = call(
                functools.partial(relay_kernel, j),
                "relay",
                [(cells, inner)],
                [landed[g]] + before,
                any_last=len(before),
            )
            pieces.append(step_to(relayed[0], j))
        (block,) = call(functools.partial(gather_kernel, count), "gather", [block_shape], pieces)
        others = from_sides(block, sides)
        if step < clips - 1:
            done += call(
                functools.partial(space_clip_kernel, g, count, sides),
                "space_clip",
                [block_shape],
                [block] + others + clip_sides + space_weights + (done[step - 1 :] if step else []),
                any_last=len(done[step - 1 :]) if step else 0,
                mebibytes=room,
                flops=project,
            )
    own = call(
        functools.partial(space_own_kernel, order[-1], count),
        "space_own",
        [block_shape] * 3,
        [block, rows] + space_weights,
        mebibytes=room,
        flops=project // 2,
    )
    (spatial,) = call(
        functools.partial(space_last_kernel, order, count, sides - 1),
        "space_last",
        [(clips, patches, inner)],
        others + clip_sides[1:] + space_weights + own + done,
        mebibytes=room,
        flops=project // 2,
    )
    return spatial.reshape(clips, 1, patches, inner)


def solution(mesh):
    sizes = (mesh.shape["frame"], mesh.shape["patch"])
    in_specs = (P(None, "frame", "patch", None),) + (P(),) * 9
    out_specs = P(None, "frame", "patch", None)
    return jax.shard_map(
        functools.partial(body, sizes),
        mesh=mesh,
        in_specs=in_specs,
        out_specs=out_specs,
        check_vma=False,
    )
```

```python
import functools

import jax
import jax.numpy as jnp
from jax import lax
from jax.experimental import pallas as pl
from jax.experimental.pallas import tpu as pltpu
from jax.sharding import PartitionSpec as P

HDIM = 80
LANES = 128
EPS = 1e-06
CELLS = 16
MIB = 1024 * 1024

VMEM = pl.BlockSpec(memory_space=pltpu.VMEM)
ANY = pl.BlockSpec(memory_space=pl.ANY)


def layer_norm(values, norm_gain):
    average = jnp.mean(values, axis=-1, keepdims=True)
    centred = values - average
    variance = jnp.mean(centred * centred, axis=-1, keepdims=True)
    return (centred * lax.rsqrt(variance + EPS) * norm_gain).astype(jnp.bfloat16)


def head_norm(part, gain, heads):
    sums = lax.dot_general(
        (part * part).astype(jnp.bfloat16),
        heads[:LANES],
        (((1,), (1,)), ((), ())),
        preferred_element_type=jnp.float32,
    )
    inverse = lax.rsqrt(sums * (1.0 / HDIM) + EPS)
    high = inverse.astype(jnp.bfloat16)
    low = (inverse - high.astype(jnp.float32)).astype(jnp.bfloat16)
    scale = jnp.dot(
        jnp.concatenate([high, low], axis=1), heads, preferred_element_type=jnp.float32
    )
    return (part * scale * gain).astype(jnp.bfloat16)


def lanes_of(head, tile, rows):
    lane = lax.broadcasted_iota(jnp.int32, (rows, LANES), 1) + tile * LANES
    return (lane >= head * HDIM) & (lane < (head + 1) * HDIM)


def attend(query, load_keys, load_values, inner, keep):
    rows = query.shape[0]
    spans, masks, scores, exponents, totals = [], [], [], [], []
    for head in range(inner // HDIM):
        first, last = head * HDIM // LANES, ((head + 1) * HDIM - 1) // LANES
        spans.append((first, last + 1))
        masks.append([lanes_of(head, tile, rows) for tile in range(first, last + 1)])
        own = [
            jnp.where(mask, query[:, t * LANES : (t + 1) * LANES], jnp.zeros((), query.dtype))
            for mask, t in zip(masks[-1], range(first, last + 1))
        ]
        keys = load_keys(first * LANES, (last + 1) * LANES)
        scores.append(
            lax.dot_general(
                jnp.concatenate(own, axis=1),
                keys,
                (((1,), (1,)), ((), ())),
                preferred_element_type=jnp.float32,
            )
        )
    for score in scores:
        exponent = jnp.exp(score * HDIM ** (-0.5))
        if keep is not None:
            exponent = jnp.where(keep, exponent, 0.0)
        totals.append(jnp.sum(exponent, axis=-1, keepdims=True))
        exponents.append(exponent.astype(jnp.bfloat16))
    tiles = [None] * (inner // LANES)
    for (first, end), mask, exponent, total in zip(spans, masks, exponents, totals):
        values = load_values(first * LANES, end * LANES)
        summed = jnp.dot(exponent, values, preferred_element_type=jnp.float32)
        result = summed * (1.0 / total)
        for i, t in enumerate(range(first, end)):
            piece = result[:, i * LANES : (i + 1) * LANES]
            tiles[t] = piece if tiles[t] is None else jnp.where(mask[i], piece, tiles[t])
    return jnp.concatenate(tiles, axis=1)


def partner_rows(k, cells):
    chip = lax.axis_index("frame") // 2
    return pl.ds(pl.multiple_of((chip ^ k) * cells, cells), cells)


def pack_kernel(cells, x_ref, *out_refs):
    for k, out_ref in enumerate(out_refs):
        out_ref[...] = x_ref[partner_rows(k, cells), :]


def time_kernel(count, *refs):
    pieces, weights, (q_ref, kv_ref) = refs[:count], refs[count : count + 5], refs[-2:]
    norm_ref, w_ref, qg_ref, kg_ref, heads_ref = weights
    inner = w_ref.shape[1] // 3
    normed = jnp.concatenate(
        [layer_norm(ref[...].astype(jnp.float32), norm_ref[...]) for ref in pieces], axis=0
    )
    product = jnp.dot(normed, w_ref[...], preferred_element_type=jnp.float32)
    query = head_norm(product[:, :inner], qg_ref[...], heads_ref[...])
    keys = head_norm(product[:, inner : 2 * inner], kg_ref[...], heads_ref[...])
    shape = q_ref.shape
    q_ref[...] = query.reshape(shape)
    kv_ref[0] = keys.reshape(shape)
    kv_ref[1] = product[:, 2 * inner :].astype(jnp.bfloat16).reshape(shape)


def time_attention_kernel(parts, *refs):
    queries, held, outs = refs[:2], refs[2:6], refs[7:]
    count, cells, inner = outs[0].shape
    rows = count * len(outs) * CELLS
    row = lax.broadcasted_iota(jnp.int32, (rows, 2 * rows), 0)
    col = lax.broadcasted_iota(jnp.int32, (rows, 2 * rows), 1)
    keep = lax.rem(row, CELLS) == lax.rem(col, CELLS)
    for b in range(cells // CELLS):
        at = slice(b * CELLS, (b + 1) * CELLS)
        query = jnp.concatenate([ref[:, at, :] for ref in queries], axis=0).reshape(rows, inner)

        def load(which):
            def columns(lo, hi):
                blocks = [ref[which, :, at, lo:hi] for ref in held]
                return jnp.concatenate(blocks, axis=0).reshape(2 * rows, hi - lo)

            return columns

        result = attend(query, load(0), load(1), inner, keep).astype(jnp.bfloat16)
        for i, k in enumerate(parts[0] + parts[1]):
            outs[k // count][k % count, at, :] = result[i * CELLS : (i + 1) * CELLS]


def gather_kernel(count, *refs):
    pieces, out_ref = refs[:count], refs[-1]
    cells = pieces[0].shape[0]
    chip = lax.axis_index("frame") // 2
    for j, ref in enumerate(pieces):
        at = lax.rem(chip, count) ^ j
        out_ref[pl.ds(pl.multiple_of(at * cells, cells), cells), :] = ref[...]


def relay_kernel(which, landed_ref, *refs):
    refs[-1][...] = landed_ref[which]


def clip_of(group, count):
    return (lax.axis_index("frame") // 2 // count) ^ group


def space_rows(blocks, clips, where, with_query, weights):
    wo_ref, norm_ref, w_ref, qg_ref, kg_ref, heads_ref = weights
    patches, inner = blocks[0].shape
    at = pl.ds(pl.multiple_of(where * patches, patches), patches)
    normed = []
    for block, clip_ref in zip(blocks, clips):
        delta = jnp.dot(block[...], wo_ref[...], preferred_element_type=jnp.float32)
        own = clip_ref[at, :].astype(jnp.float32)
        mixed = (own + delta).astype(jnp.bfloat16).astype(jnp.float32)
        normed.append(layer_norm(mixed, norm_ref[...]))
    query = None
    if with_query:
        product = jnp.dot(normed[0], w_ref[:, :inner], preferred_element_type=jnp.float32)
        query = head_norm(product, qg_ref[...], heads_ref[...])
    normed = jnp.concatenate(normed, axis=0)
    product = jnp.dot(normed, w_ref[:, inner:], preferred_element_type=jnp.float32)
    keys = head_norm(product[:, :inner], kg_ref[...], heads_ref[...])
    return query, keys, product[:, inner:].astype(jnp.bfloat16)


def space_clip_kernel(group, count, sides, *refs):
    blocks, clips, refs = refs[:sides], refs[sides : 2 * sides], refs[2 * sides :]
    weights, out_ref = refs[:6], refs[-1]
    query, keys, values = space_rows(blocks, clips, clip_of(group, count), True, weights)
    inner = out_ref.shape[1]
    result = attend(
        query, lambda lo, hi: keys[:, lo:hi], lambda lo, hi: values[:, lo:hi], inner, None
    )
    out_ref[...] = result.astype(jnp.bfloat16)


def space_own_kernel(group, count, block_ref, clip_ref, *refs):
    weights, (q_ref, k_ref, v_ref) = refs[:6], refs[6:]
    q_ref[...], k_ref[...], v_ref[...] = space_rows(
        [block_ref], [clip_ref], clip_of(group, count), True, weights
    )


def space_last_kernel(order, count, others, *refs):
    blocks, clips, refs = refs[:others], refs[others : 2 * others], refs[2 * others :]
    weights, own, done, out_ref = refs[:6], refs[6:9], refs[9:-1], refs[-1]
    inner = out_ref.shape[2]
    for g, ref in zip(order, done):
        out_ref[clip_of(g, count)] = ref[...]
    where = clip_of(order[-1], count)
    _, keys, values = space_rows(blocks, clips, where, False, weights)
    q_ref, k_ref, v_ref = own
    result = attend(
        q_ref[...],
        lambda lo, hi: jnp.concatenate([k_ref[:, lo:hi], keys[:, lo:hi]], axis=0),
        lambda lo, hi: jnp.concatenate([v_ref[:, lo:hi], values[:, lo:hi]], axis=0),
        inner,
        None,
    )
    out_ref[where] = result.astype(jnp.bfloat16)


def from_sides(array, size):
    return [
        lax.ppermute(array, "patch", [(i, (i - hop) % size) for i in range(size)])
        for hop in range(1, size)
    ]


def call(kernel, name, outs, operands, any_last=0, scratch=(), mebibytes=20, flops=0):
    bf16 = jnp.bfloat16
    shapes = [jax.ShapeDtypeStruct(shape, bf16) for shape in outs]
    results = pl.pallas_call(
        kernel,
        out_shape=shapes,
        in_specs=[VMEM] * (len(operands) - any_last) + [ANY] * any_last,
        out_specs=[VMEM] * len(outs),
        scratch_shapes=[pltpu.VMEM(shape, bf16) for shape in scratch],
        compiler_params=pltpu.CompilerParams(vmem_limit_bytes=mebibytes * MIB),
        cost_estimate=pl.CostEstimate(flops=flops, bytes_accessed=MIB, transcendentals=0),
        name=name,
    )(*operands)
    return list(results)


def body(
    sizes,
    clip,
    norm_time,
    w_time_qkv,
    q_gain_time,
    k_gain_time,
    w_time_out,
    norm_space,
    w_space_qkv,
    q_gain_space,
    k_gain_space,
):
    frames, sides = sizes
    clips, _, patches, features = clip.shape
    inner = w_time_out.shape[0]
    tokens = clips * patches
    chips = frames // 2
    cells = tokens // chips
    half = chips // 2
    count = chips // clips
    bf16 = jnp.bfloat16
    lane = jnp.arange(2 * LANES) % LANES
    heads = (lane[:, None] == jnp.arange(inner)[None, :] // HDIM).astype(bf16)
    quarter = max(1, half // 2)
    parts = [
        list(range(quarter)) + list(range(half, half + quarter)),
        list(range(half + quarter, chips)) + list(range(quarter, half)),
    ]
    order = list(range(clips))
    project = 2 * (tokens // 2) * features * 3 * inner * 2

    def exchange(pieces):
        moved = {0: pieces[0]}
        for k in parts[0] + parts[1]:
            if k:
                pairs = [(i, i ^ (2 * k)) for i in range(frames)]
                moved[k] = lax.ppermute(pieces[k], "frame", pairs)
        return moved

    def other_core(array):
        return lax.ppermute(array, "frame", [(i, i ^ 1) for i in range(frames)])

    rows = clip.reshape(tokens, features)
    clip_sides = [rows] + from_sides(rows, sides)
    pieces = call(
        functools.partial(pack_kernel, cells), "pack", [(cells, features)] * chips, [rows]
    )
    moved = exchange(pieces)

    time_weights = [
        norm_time.reshape(1, -1),
        w_time_qkv,
        q_gain_time.reshape(1, -1),
        k_gain_time.reshape(1, -1),
        heads,
    ]
    queries, held = [], []
    for members, name in zip(parts, ("time_first", "time_second")):
        query, key_value = call(
            functools.partial(time_kernel, len(members)),
            name,
            [(len(members), cells, inner), (2, len(members), cells, inner)],
            [moved[k] for k in members] + time_weights + queries,
            any_last=len(queries),
            flops=project,
        )
        queries.append(query)
        held += [key_value, other_core(key_value)]
    attended = call(
        functools.partial(time_attention_kernel, parts),
        "time_attention",
        [(count, cells, inner)] * clips,
        queries + held + [clip_sides[-1]],
        any_last=1,
        flops=project,
    )

    def step_to(array, k):
        return lax.ppermute(array, "frame", [(i, i ^ (2 * k)) for i in range(frames)])

    landed = {g: step_to(attended[g], g * count) if g else attended[0] for g in order}
    space_weights = [
        w_time_out,
        norm_space.reshape(1, -1),
        w_space_qkv,
        q_gain_space.reshape(1, -1),
        k_gain_space.reshape(1, -1),
        heads,
    ]
    room = 24 + 8 * (sides - 2)
    block_shape = (patches, inner)
    done = []
    for step, g in enumerate(order):
        pieces = [landed[g][0]]
        before = done[1:2] if step >= 2 else []
        for j in range(1, count):
            relayed = call(
                functools.partial(relay_kernel, j),
                "relay",
                [(cells, inner)],
                [landed[g]] + before,
                any_last=len(before),
            )
            pieces.append(step_to(relayed[0], j))
        (block,) = call(functools.partial(gather_kernel, count), "gather", [block_shape], pieces)
        others = from_sides(block, sides)
        if step < clips - 1:
            done += call(
                functools.partial(space_clip_kernel, g, count, sides),
                "space_clip",
                [block_shape],
                [block] + others + clip_sides + space_weights + (done[step - 1 :] if step else []),
                any_last=len(done[step - 1 :]) if step else 0,
                mebibytes=room,
                flops=project,
            )
    own = call(
        functools.partial(space_own_kernel, order[-1], count),
        "space_own",
        [block_shape] * 3,
        [block, rows] + space_weights,
        mebibytes=room,
        flops=project // 2,
    )
    (spatial,) = call(
        functools.partial(space_last_kernel, order, count, sides - 1),
        "space_last",
        [(clips, patches, inner)],
        others + clip_sides[1:] + space_weights + own + done,
        mebibytes=room,
        flops=project // 2,
    )
    return spatial.reshape(clips, 1, patches, inner)


def solution(mesh):
    sizes = (mesh.shape["frame"], mesh.shape["patch"])
    in_specs = (P(None, "frame", "patch", None),) + (P(),) * 9
    out_specs = P(None, "frame", "patch", None)
    return jax.shard_map(
        functools.partial(body, sizes),
        mesh=mesh,
        in_specs=in_specs,
        out_specs=out_specs,
        check_vma=False,
    )
```
